128 devices in a mesh: row: 8 (over z_lo, x), col: 16 (over z_hi, y, core).
Axes of the slice: x: 4, y: 4, z: 4 (z_hi: 2, z_lo: 2; z = z_hi * 2 + z_lo), core: 2. Of those that a mesh axis runs over, the one named last changes fastest.
Arguments:
- stored: bfloat16 [16, 16, 12, 128, 128], P('row', 'col'), may hold values from -1.75 to 1.75
- block_cols: int32 [16, 16, 12], replicated, may hold values from 0 to 11, as said below
- out_cols: int32 [16, 16, 12, 8], P('row', 'col'), may hold values from 0 to 11, as said below
Outputs:
- window: bfloat16 [16, 16, 12, 8, 128, 128], P('row', 'col')
The draws below stay inside these ranges and needn't reach their ends.
Inputs may be any that keep to these rules, and one draw needn't show every extreme that they name: Each block_cols[v, w, :] names every block column of its group exactly once. `out_cols`: every listed column receives at least one block product of the window; a column may be listed twice in one row.
All inputs are finite; a program needn't handle non-finite values.
Results may differ from the reference program's by a relative error of at most 0.001.
Values may be sent and summed in bfloat16 or wider, within the bound.
No kernel may reach another device: no remote copies, remote signals or barrier semaphores. Data moves between devices by JAX's collectives and lax.ppermute only.
A program may use at most 128 MiB of HBM per device.

```python
import jax
import jax.numpy as jnp
from jax import lax

BLOCK = 128
TILE_BLOCKS = 12
STEPS = 4
KEPT = 8
GRID = 16


def block_pattern(key):
    key_list = jax.random.split(key, GRID * GRID)
    orderings = jax.vmap(lambda subkey: jax.random.permutation(subkey, TILE_BLOCKS))(key_list)
    return orderings.reshape(GRID, GRID, TILE_BLOCKS).astype(jnp.int32)


def draw_block_cols(key, part):
    return block_pattern(key)


def draw_out_cols(key, part):
    pattern = block_pattern(key)
    key = jax.random.fold_in(key, 5)
    inverses = jnp.argsort(pattern, axis=-1).astype(jnp.int32)
    tile_rows = jnp.arange(GRID, dtype=jnp.int32)[:, None]
    tile_cols = jnp.arange(GRID, dtype=jnp.int32)[None, :]
    hit_cols = []
    for window_step in range(STEPS):
        ahead = (tile_rows + tile_cols + window_step) % GRID
        left_cols = pattern[tile_rows, ahead]
        left_inverse = inverses[ahead, tile_rows]
        right_cols = pattern[ahead, tile_cols]
        right_inverse = inverses[tile_cols, ahead]
        hit_cols.append(jnp.take_along_axis(right_cols, left_cols, axis=-1))
        hit_cols.append(jnp.take_along_axis(right_inverse, left_cols, axis=-1))
        hit_cols.append(jnp.take_along_axis(right_cols, left_inverse, axis=-1))
        hit_cols.append(jnp.take_along_axis(right_inverse, left_inverse, axis=-1))
    stacked = jnp.stack(hit_cols, -1)
    scores = jax.random.randint(key, stacked.shape, 0, 1 << 16) * (4 * STEPS) + jnp.arange(4 * STEPS, dtype=jnp.int32)
    unused_values, chosen = lax.top_k(scores, KEPT)
    return jnp.take_along_axis(stacked, chosen, axis=-1).astype(jnp.int32)


def steps_of(key, shape, pieces, least, high):
    loudness, own = 1.0, jax.random.fold_in(key, 6)
    for axis_at, shards_of in pieces:
        steps = jnp.exp(jax.random.uniform(jax.random.fold_in(own, axis_at), (shards_of,), jnp.float32, least / len(pieces), high / len(pieces)))
        loudness = loudness * jnp.repeat(steps, shape[axis_at] // shards_of).reshape([-1 if axis == axis_at else 1 for axis in range(len(shape))])
    return loudness


def noise(key, shape, scale, bound, pieces=(), kind=jnp.bfloat16):
    factor_of = steps_of(key, shape, pieces, -0.22, 0.18) if pieces else 1.0
    entries = jax.random.normal(key, shape, jnp.float32) * scale * factor_of
    return jnp.minimum(jnp.maximum(entries, -bound), bound).astype(kind)


def setup_inputs(seed: int = 0) -> dict:
    splits = jax.random.split(jax.random.key(seed), 4)
    return {
        "stored": noise(splits[0], (GRID, GRID, TILE_BLOCKS, BLOCK, BLOCK), (BLOCK ** -0.25), 1.75, ((0, 8), (1, 16))),
        "block_cols": draw_block_cols(jax.random.fold_in(splits[3], 71), 0),
        "out_cols": draw_out_cols(jax.random.fold_in(splits[3], 71), 0),
    }


def inverse(ordering):
    length = ordering.shape[0]
    return jnp.zeros((length,), jnp.int32).at[ordering].set(jnp.arange(length, dtype=jnp.int32))


def tile_terms(own_left, mirror_left, own_right, mirror_right, left_cols, left_inverse, right_cols, right_inverse, kept_cols):
    mirror_rows = jnp.take(mirror_left, left_inverse, axis=0)
    lead_mirror = jnp.take(right_inverse, left_cols)
    tail_mirror = jnp.take(right_inverse, left_inverse)
    highest = lax.Precision.HIGHEST
    products = jnp.stack([
        jnp.einsum("ipq,iqr->ipr", own_left, jnp.take(own_right, left_cols, axis=0), precision=highest),
        jnp.einsum("ipq,irq->ipr", own_left, jnp.take(mirror_right, lead_mirror, axis=0), precision=highest),
        jnp.einsum("iqp,iqr->ipr", mirror_rows, jnp.take(own_right, left_inverse, axis=0), precision=highest),
        jnp.einsum("iqp,irq->ipr", mirror_rows, jnp.take(mirror_right, tail_mirror, axis=0), precision=highest)], 0)
    columns = jnp.stack([jnp.take(right_cols, left_cols), lead_mirror, jnp.take(right_cols, left_inverse), tail_mirror], 0)
    weights = (columns[:, :, None] == kept_cols[None]).astype(jnp.float32)
    return jnp.einsum("cik,cipr->ikpr", weights, products, precision=highest)


def reference(stored, block_cols, out_cols):
    grid_side = block_cols.shape[0]
    row_count = block_cols.shape[2]
    block_side = stored.shape[3]
    kept_count = out_cols.shape[3]
    inverses = jax.vmap(jax.vmap(inverse))(block_cols)

    def one_tile(flat_index):
        tile_row = flat_index // grid_side
        tile_col = flat_index % grid_side
        kept_cols = out_cols[tile_row, tile_col]
        accumulated = jnp.zeros((row_count, kept_count, block_side, block_side), jnp.float32)
        for window_step in range(STEPS):
            ahead = (tile_row + tile_col + window_step) % grid_side
            accumulated = accumulated + tile_terms(
                stored[tile_row, ahead].astype(jnp.float32),
                stored[ahead, tile_row].astype(jnp.float32),
                stored[ahead, tile_col].astype(jnp.float32),
                stored[tile_col, ahead].astype(jnp.float32),
                block_cols[tile_row, ahead], inverses[ahead, tile_row],
                block_cols[ahead, tile_col], inverses[tile_col, ahead], kept_cols)
        return accumulated.astype(jnp.bfloat16)

    result = lax.map(one_tile, jnp.arange(grid_side * grid_side, dtype=jnp.int32))
    return result.reshape(grid_side, grid_side, row_count, kept_count, block_side, block_side)
```

```python
import functools

import jax
import jax.numpy as jnp
import numpy as np
from jax import lax
from jax.experimental import pallas as pl
from jax.experimental.pallas import tpu as pltpu
from jax.sharding import PartitionSpec as P

STEPS = 4
GRID = 16
ROWS = 8
COLS = 16
DEVICES = ROWS * COLS
AXES = ("row", "col")
TILE = 12
SIDE = 128
PIECE = 24
HOLDERS = 64

RIGHT_OWN, RIGHT_MIRROR, LEFT_OWN, LEFT_MIRROR = 0, 6, 12, 24
SLOTS = 36
CENTRE = (2, 3)
OUTER = (0, 1, 4, 5)


def slot_of(kind, rel, lead=0):
    return kind + (2 * rel + lead if kind in (LEFT_OWN, LEFT_MIRROR) else rel)


def centre_left(core):
    if core == 0:
        return ((LEFT_MIRROR, 3, 0), (LEFT_OWN, 3, 1), (LEFT_MIRROR, 3, 1), (LEFT_OWN, 2, 1))
    return ((LEFT_MIRROR, 2, 1), (LEFT_OWN, 2, 0), (LEFT_MIRROR, 2, 0), (LEFT_OWN, 3, 0))


def mirror_rels(core, high):
    return tuple(core + high + i for i in range(4))


def own_rels(core, high):
    rest = [rel for rel in mirror_rels(core, high) if rel not in CENTRE]
    return tuple(sorted(rest, key=lambda rel: rel % 2))


def shifted(tiles, by):
    return [(kind, rel + by, lead) for kind, rel, lead in tiles]


def from_neighbours(core):
    by = 2 * core * 2 - 2
    return shifted(centre_left(core)[:3], by), shifted(centre_left(1 - core)[1:], by)


def centre_slots(core, high):
    tiles = [(RIGHT_OWN, rel) for rel in CENTRE]
    tiles += [(RIGHT_MIRROR, rel) for rel in mirror_rels(core, high)]
    tiles += centre_left(core) + centre_left(1 - core)
    return [slot_of(*tile) for tile in tiles]


def outer_slots(core, high):
    tiles = [(RIGHT_OWN, rel) for rel in own_rels(core, high)]
    tiles += [(RIGHT_MIRROR, rel) for rel in mirror_rels(core, high)]
    missing = core if high else core + 4
    tiles += [(RIGHT_OWN, missing), (RIGHT_MIRROR, missing)]
    first, second = from_neighbours(core)
    tiles += first + second
    first, second = from_neighbours(1 - core)
    tiles += [first[0], second[2]]
    return [slot_of(*tile) for tile in tiles]


def slot_table(slots):
    return np.array([slots(core, high) for core in (0, 1) for high in (0, 1)], np.int32)


def source_of(tile, row, col):
    kind, rel, lead = tile
    ahead = (2 * row + 2 * (col // 2) + rel) % GRID
    own = 2 * row + lead
    lead, tail = {
        RIGHT_OWN: (ahead, col),
        RIGHT_MIRROR: (col, ahead),
        LEFT_OWN: (own, ahead),
        LEFT_MIRROR: (ahead, own),
    }[kind]
    return lead // 2 * COLS + tail, lead % 2


PAIRS = 5


def routes():
    table = np.zeros((2, DEVICES, PAIRS), np.int32)
    for device in range(DEVICES):
        row, col = divmod(device, COLS)
        core, high = col % 2, row % 2
        wanted = [[None] * PAIRS, [None] * PAIRS]
        for i in range(4):
            wanted[core][i] = (RIGHT_MIRROR, mirror_rels(core, high)[i], 0)
            wanted[1 - core][i] = centre_left(core)[i]
        for i in range(2):
            wanted[i][4] = (RIGHT_OWN, own_rels(core, high)[i], 0)
        for half in range(2):
            for pair in range(PAIRS):
                source, held = source_of(wanted[half][pair], row, col)
                assert held == half
                table[half, device, pair] = source
    return table


def pick_kernel(route_ref, held_ref, out_ref):
    group, pairs = out_ref.shape[:2]
    base = pl.program_id(0) * group * pairs

    def body(target, carry):
        for pair in range(pairs):
            out_ref[target, pair] = held_ref[route_ref[base + target * pairs + pair]]
        return carry

    lax.fori_loop(0, group, body, 0, unroll=4)


def pick(route, held):
    group = 16
    return pl.pallas_call(
        pick_kernel,
        grid_spec=pltpu.PrefetchScalarGridSpec(
            num_scalar_prefetch=1,
            grid=(DEVICES // group,),
            in_specs=[pl.BlockSpec((DEVICES, PIECE, SIDE), lambda t, *_: (0, 0, 0))],
            out_specs=pl.BlockSpec((group, PAIRS, PIECE, SIDE), lambda t, *_: (t, 0, 0, 0)),
        ),
        out_shape=jax.ShapeDtypeStruct((DEVICES, PAIRS, PIECE, SIDE), jnp.bfloat16),
        compiler_params=pltpu.CompilerParams(vmem_limit_bytes=16 << 20),
        cost_estimate=pl.CostEstimate(
            flops=0, bytes_accessed=2 * DEVICES * PAIRS * PIECE * SIDE * 2, transcendentals=0
        ),
    )(route, held)


def matmul(left, right, right_dim):
    return lax.dot_general(
        left, right, (((1,), (right_dim,)), ((), ())), preferred_element_type=jnp.float32
    )


def product_kernel(sources, last, cols_ref, kept_ref, place_ref, slot_ref, *refs):
    arrays, refs = refs[:sources], refs[sources:]
    if last:
        partial_ref, refs = refs[0], refs[1:]
    out_ref, tiles, total, right_inv, left_inv, sems = refs
    step = pl.program_id(0)
    slot, line = step // TILE, step % TILE
    row, col = place_ref[0], place_ref[1]
    core = col % 2
    first = 2 * row + col - core

    def group(rel):
        return (first + rel) % GRID

    def entry(lead, tail, line):
        return cols_ref[(lead * GRID + tail) * TILE + line]

    @pl.when(step == 0)
    def _():
        started = []
        for source in arrays:
            for position in range(source.shape[0]):
                index = len(started)
                started.append(
                    pltpu.make_async_copy(
                        source.at[position], tiles.at[slot_ref[index]], sems.at[index]
                    )
                )
        for copy in started:
            copy.start()
        for rel in OUTER if last else CENTRE:
            ahead = group(rel)
            for q in range(TILE):
                right_inv[rel * TILE + entry(col, ahead, q)] = q
                for half in range(2):
                    left_inv[(2 * rel + half) * TILE + entry(ahead, 2 * row + half, q)] = q
        for copy in started:
            copy.wait()

    total[...] = jnp.zeros_like(total)
    if last:
        edge = slot + core
        rels = (jnp.where(edge == 2, 4, edge), jnp.where(edge == 0, 1, 3 + edge))
    else:
        rels = CENTRE
    terms = []
    for rel in rels:
        ahead = group(rel)
        own_col = entry(2 * row + slot, ahead, line)
        mirror_col = left_inv[(2 * rel + slot) * TILE + line]
        own = tiles[LEFT_OWN + 2 * rel + slot, line]
        mirror = tiles[LEFT_MIRROR + 2 * rel + slot, mirror_col].T
        for left, middle in ((own, own_col), (mirror, mirror_col)):
            flipped = right_inv[rel * TILE + middle]
            terms.append(
                (entry(ahead, col, middle), matmul(left, tiles[RIGHT_OWN + rel, middle], 0))
            )
            terms.append((flipped, matmul(left, tiles[RIGHT_MIRROR + rel, flipped], 1)))
    for target, term in terms:
        total[target] += term
    kept_count = out_ref.shape[3]
    for o in range(kept_count):
        value = total[kept_ref[step * kept_count + o]]
        if last:
            value = value + partial_ref[0, 0, 0, o]
        out_ref[0, 0, 0, o] = value.astype(out_ref.dtype)


def products(cols, kept, place, slots, arrays, kept_count, partial=None):
    last = partial is not None
    copies = sum(a.shape[0] for a in arrays)
    block = pl.BlockSpec(
        (1, 1, 1, kept_count, SIDE, SIDE), lambda t, *_: (t // TILE, 0, t % TILE, 0, 0, 0)
    )
    dtype = jnp.bfloat16 if last else jnp.float32
    operands = list(arrays) + ([partial] if last else [])
    return pl.pallas_call(
        functools.partial(product_kernel, len(arrays), last),
        grid_spec=pltpu.PrefetchScalarGridSpec(
            num_scalar_prefetch=4,
            grid=(2 * TILE,),
            in_specs=[pl.BlockSpec(memory_space=pl.ANY)] * len(arrays) + [block] * last,
            out_specs=block,
            scratch_shapes=[
                pltpu.VMEM((SLOTS, TILE, SIDE, SIDE), jnp.bfloat16),
                pltpu.VMEM((TILE, SIDE, SIDE), jnp.float32),
                pltpu.SMEM((6 * TILE,), jnp.int32),
                pltpu.SMEM((12 * TILE,), jnp.int32),
                pltpu.SemaphoreType.DMA((copies,)),
            ],
        ),
        out_shape=jax.ShapeDtypeStruct((2, 1, TILE, kept_count, SIDE, SIDE), dtype),
        compiler_params=pltpu.CompilerParams(vmem_limit_bytes=28 << 20),
        cost_estimate=pl.CostEstimate(
            flops=192 * 2 * SIDE**3, bytes_accessed=25 << 20, transcendentals=0
        ),
    )(cols, kept, place, slots, *operands)


def moved(tiles, target):
    pairs = []
    for row in range(ROWS):
        for col in range(COLS):
            to_row, to_chip, to_core = target(row, col // 2, col % 2)
            to = to_row % ROWS * COLS + 2 * (to_chip % (COLS // 2)) + to_core
            pairs.append((row * COLS + col, to))
    return lax.ppermute(tiles, AXES, pairs)


def one(tiles, index):
    return lax.dynamic_slice_in_dim(tiles, index, 1, 0)


def on_device(stored, block_cols, out_cols):
    row, col = lax.axis_index("row"), lax.axis_index("col")
    core, high = col % 2, row % 2
    half = (row * COLS + col) // HOLDERS
    own_centre = moved(stored[:, 0], lambda r, m, c: (r - m - 1, m, c))
    spread = stored.reshape(DEVICES, PIECE, SIDE)
    held = lax.all_to_all(spread, AXES, split_axis=0, concat_axis=0, tiled=True)
    own_across = moved(one(own_centre, core), lambda r, m, c: (r ^ 1, m, c))
    route = jnp.asarray(routes().reshape(2, -1))[half]
    outgoing = pick(route, held)
    received = lax.all_to_all(outgoing, AXES, split_axis=0, concat_axis=0, tiled=True)
    received = received.reshape(2, HOLDERS, PAIRS, PIECE, SIDE)

    def gathered(pieces, count):
        return pieces[0, :, :count].transpose(1, 0, 2, 3).reshape(count, TILE, SIDE, SIDE)

    left = gathered(one(received, 1 - core), 4)
    forward = moved(left[:3], lambda r, m, c: (r, m + 1 - 2 * c, c))
    backward = moved(left[1:], lambda r, m, c: (r, m - 1 + 2 * c, 1 - c))
    sibling = moved(left, lambda r, m, c: (r, m, 1 - c))
    mirror = gathered(one(received, core), 4)
    mirror_across = moved(one(mirror, 2 - high), lambda r, m, c: (r ^ 1, m, c))
    own_outer = received[:, :, 4].reshape(2, TILE, SIDE, SIDE)
    shared = moved(
        jnp.concatenate([forward[:1], backward[2:]], 0), lambda r, m, c: (r, m, 1 - c)
    )
    which = 2 * core + high
    place = jnp.stack([row, col]).astype(jnp.int32)
    cols, kept = block_cols.reshape(-1), out_cols.reshape(-1)
    kept_count = out_cols.shape[3]
    partial = products(
        cols,
        kept,
        place,
        jnp.asarray(slot_table(centre_slots))[which],
        (own_centre, mirror, left, sibling),
        kept_count,
    )
    return products(
        cols,
        kept,
        place,
        jnp.asarray(slot_table(outer_slots))[which],
        (own_outer, mirror, own_across, mirror_across, forward, backward, shared),
        kept_count,
        partial,
    )


def solution(mesh):
    placed = (P("row", "col", None, None, None), P(), P("row", "col", None, None))
    return jax.shard_map(
        on_device,
        mesh=mesh,
        in_specs=placed,
        out_specs=P("row", "col", None, None, None, None),
        check_vma=False,
    )
```

```python
import functools

import jax
import jax.numpy as jnp
import numpy as np
from jax import lax
from jax.experimental import pallas as pl
from jax.experimental.pallas import tpu as pltpu
from jax.sharding import PartitionSpec as P

STEPS = 4
GRID = 16
ROWS = 8
COLS = 16
DEVICES = ROWS * COLS
AXES = ("row", "col")
TILE = 12
SIDE = 128
PIECE = 24
HOLDERS = 64

RIGHT_OWN, RIGHT_MIRROR, LEFT_OWN, LEFT_MIRROR = 0, 6, 12, 24
SLOTS = 36
CENTRE = (2, 3)
OUTER = (0, 1, 4, 5)


def slot_of(kind, rel, lead=0):
    return kind + (2 * rel + lead if kind in (LEFT_OWN, LEFT_MIRROR) else rel)


def centre_left(core):
    if core == 0:
        return ((LEFT_MIRROR, 3, 0), (LEFT_OWN, 3, 1), (LEFT_MIRROR, 3, 1), (LEFT_OWN, 2, 1))
    return ((LEFT_MIRROR, 2, 1), (LEFT_OWN, 2, 0), (LEFT_MIRROR, 2, 0), (LEFT_OWN, 3, 0))


def mirror_rels(core, high):
    return tuple(core + high + i for i in range(4))


def own_rels(core, high):
    rels = mirror_rels(core, high)
    return tuple(sorted(rels[:2], key=lambda rel: rel % 2)) + tuple(
        sorted(rels[2:], key=lambda rel: rel % 2)
    )


def shifted(tiles, by):
    return [(kind, rel + by, lead) for kind, rel, lead in tiles]


def from_neighbours(core):
    by = 2 * core * 2 - 2
    return shifted(centre_left(core)[:3], by), shifted(centre_left(1 - core)[1:], by)


def rights(array, kind, held, wanted):
    return [(array, held.index(rel), slot_of(kind, rel)) for rel in held if rel in wanted]


def centre_copies(core, high):
    copies = rights(0, RIGHT_OWN, own_rels(core, high), CENTRE)
    copies += rights(1, RIGHT_MIRROR, mirror_rels(core, high), CENTRE)
    copies += [(2, i, slot_of(*tile)) for i, tile in enumerate(centre_left(core))]
    copies += [(3, i, slot_of(*tile)) for i, tile in enumerate(centre_left(1 - core))]
    return copies


def outer_copies(core, high):
    copies = rights(0, RIGHT_OWN, own_rels(core, high), OUTER)
    copies += rights(1, RIGHT_MIRROR, mirror_rels(core, high), OUTER)
    missing = core if high else core + 4
    copies += [(2, 0, slot_of(RIGHT_OWN, missing)), (2, 1, slot_of(RIGHT_MIRROR, missing))]
    first, second = from_neighbours(core)
    copies += [(3, i, slot_of(*tile)) for i, tile in enumerate(first)]
    copies += [(4, i, slot_of(*tile)) for i, tile in enumerate(second)]
    first, second = from_neighbours(1 - core)
    copies += [(5, 0, slot_of(*first[0])), (5, 1, slot_of(*second[2]))]
    return copies


def copy_arrays(copies):
    return tuple(array for array, _, _ in copies(0, 0))


def copy_table(copies):
    table = []
    for core in (0, 1):
        for high in (0, 1):
            listed = copies(core, high)
            assert tuple(c[0] for c in listed) == copy_arrays(copies)
            table.append([c[1] for c in listed] + [c[2] for c in listed])
    return np.array(table, np.int32)


def source_of(tile, row, col):
    kind, rel, lead = tile
    ahead = (2 * row + 2 * (col // 2) + rel) % GRID
    own = 2 * row + lead
    lead, tail = {
        RIGHT_OWN: (ahead, col),
        RIGHT_MIRROR: (col, ahead),
        LEFT_OWN: (own, ahead),
        LEFT_MIRROR: (ahead, own),
    }[kind]
    return lead // 2 * COLS + tail, lead % 2


PAIRS = 6


def routes():
    table = np.zeros((2, DEVICES, PAIRS), np.int32)
    for device in range(DEVICES):
        row, col = divmod(device, COLS)
        core, high = col % 2, row % 2
        wanted = [[None] * PAIRS, [None] * PAIRS]
        for i in range(4):
            wanted[core][i] = (RIGHT_MIRROR, mirror_rels(core, high)[i], 0)
            wanted[1 - core][i] = centre_left(core)[i]
            wanted[i % 2][4 + i // 2] = (RIGHT_OWN, own_rels(core, high)[i], 0)
        for half in range(2):
            for pair in range(PAIRS):
                source, held = source_of(wanted[half][pair], row, col)
                assert held == half
                table[half, device, pair] = source
    return table


def pick_kernel(route_ref, held_ref, out_ref):
    group, pairs = out_ref.shape[:2]
    base = pl.program_id(0) * group * pairs

    def body(target, carry):
        for pair in range(pairs):
            out_ref[target, pair] = held_ref[route_ref[base + target * pairs + pair]]
        return carry

    lax.fori_loop(0, group, body, 0, unroll=4)


def pick(route, held):
    group = 16
    return pl.pallas_call(
        pick_kernel,
        grid_spec=pltpu.PrefetchScalarGridSpec(
            num_scalar_prefetch=1,
            grid=(DEVICES // group,),
            in_specs=[pl.BlockSpec((DEVICES, PIECE, SIDE), lambda t, *_: (0, 0, 0))],
            out_specs=pl.BlockSpec((group, PAIRS, PIECE, SIDE), lambda t, *_: (t, 0, 0, 0)),
        ),
        out_shape=jax.ShapeDtypeStruct((DEVICES, PAIRS, PIECE, SIDE), jnp.bfloat16),
        compiler_params=pltpu.CompilerParams(vmem_limit_bytes=16 << 20),
        cost_estimate=pl.CostEstimate(
            flops=0, bytes_accessed=2 * DEVICES * PAIRS * PIECE * SIDE * 2, transcendentals=0
        ),
    )(route, held)


def matmul(left, right, right_dim):
    return lax.dot_general(
        left, right, (((1,), (right_dim,)), ((), ())), preferred_element_type=jnp.float32
    )


def product_kernel(sources, from_arrays, last, cols_ref, kept_ref, place_ref, copy_ref, *refs):
    arrays, refs = refs[:sources], refs[sources:]
    if last:
        partial_ref, refs = refs[0], refs[1:]
    out_ref, tiles, total, right_inv, left_inv, sems = refs
    lines, kept_count = out_ref.shape[2:4]
    step = pl.program_id(0)
    slot = step * lines // TILE
    row, col = place_ref[0], place_ref[1]
    core = col % 2
    first = 2 * row + col - core

    def group(rel):
        return (first + rel) % GRID

    def entry(lead, tail, line):
        return cols_ref[(lead * GRID + tail) * TILE + line]

    @pl.when(step == 0)
    def _():
        count = len(from_arrays)
        started = [
            pltpu.make_async_copy(
                arrays[array].at[copy_ref[index]],
                tiles.at[copy_ref[count + index]],
                sems.at[index],
            )
            for index, array in enumerate(from_arrays)
        ]
        for copy in started:
            copy.start()
        for rel in OUTER if last else CENTRE:
            ahead = group(rel)
            for q in range(TILE):
                right_inv[rel * TILE + entry(col, ahead, q)] = q
                for half in range(2):
                    left_inv[(2 * rel + half) * TILE + entry(ahead, 2 * row + half, q)] = q
        for copy in started:
            copy.wait()

    total[...] = jnp.zeros_like(total)
    if last:
        edge = slot + core
        rels = (jnp.where(edge == 2, 4, edge), jnp.where(edge == 0, 1, 3 + edge))
    else:
        rels = CENTRE
    terms = []
    for sub in range(lines):
        line = step * lines % TILE + sub
        for rel in rels:
            ahead = group(rel)
            own_col = entry(2 * row + slot, ahead, line)
            mirror_col = left_inv[(2 * rel + slot) * TILE + line]
            own = tiles[LEFT_OWN + 2 * rel + slot, line]
            mirror = tiles[LEFT_MIRROR + 2 * rel + slot, mirror_col].T
            for left, middle in ((own, own_col), (mirror, mirror_col)):
                flipped = right_inv[rel * TILE + middle]
                straight = matmul(left, tiles[RIGHT_OWN + rel, middle], 0)
                terms.append((sub, entry(ahead, col, middle), straight))
                terms.append((sub, flipped, matmul(left, tiles[RIGHT_MIRROR + rel, flipped], 1)))
    for sub, target, term in terms:
        total[sub, target] += term
    for sub in range(lines):
        for o in range(kept_count):
            value = total[sub, kept_ref[(step * lines + sub) * kept_count + o]]
            if last:
                value = value + partial_ref[0, 0, sub, o]
            out_ref[0, 0, sub, o] = value.astype(out_ref.dtype)


def products(cols, kept, place, table, arrays, from_arrays, kept_count, partial=None):
    last = partial is not None
    lines = 2
    block = pl.BlockSpec(
        (1, 1, lines, kept_count, SIDE, SIDE),
        lambda t, *_: (t * lines // TILE, 0, t % (TILE // lines), 0, 0, 0),
    )
    dtype = jnp.bfloat16 if last else jnp.float32
    operands = list(arrays) + ([partial] if last else [])
    return pl.pallas_call(
        functools.partial(product_kernel, len(arrays), from_arrays, last),
        grid_spec=pltpu.PrefetchScalarGridSpec(
            num_scalar_prefetch=4,
            grid=(2 * TILE // lines,),
            in_specs=[pl.BlockSpec(memory_space=pl.ANY)] * len(arrays) + [block] * last,
            out_specs=block,
            scratch_shapes=[
                pltpu.VMEM((SLOTS, TILE, SIDE, SIDE), jnp.bfloat16),
                pltpu.VMEM((lines, TILE, SIDE, SIDE), jnp.float32),
                pltpu.SMEM((6 * TILE,), jnp.int32),
                pltpu.SMEM((12 * TILE,), jnp.int32),
                pltpu.SemaphoreType.DMA((len(from_arrays),)),
            ],
        ),
        out_shape=jax.ShapeDtypeStruct((2, 1, TILE, kept_count, SIDE, SIDE), dtype),
        compiler_params=pltpu.CompilerParams(vmem_limit_bytes=30 << 20),
        cost_estimate=pl.CostEstimate(
            flops=192 * 2 * SIDE**3, bytes_accessed=25 << 20, transcendentals=0
        ),
    )(cols, kept, place, table, *operands)


def moved(tiles, target):
    pairs = []
    for row in range(ROWS):
        for col in range(COLS):
            to_row, to_chip, to_core = target(row, col // 2, col % 2)
            to = to_row % ROWS * COLS + 2 * (to_chip % (COLS // 2)) + to_core
            pairs.append((row * COLS + col, to))
    return lax.ppermute(tiles, AXES, pairs)


def one(tiles, index):
    return lax.dynamic_slice_in_dim(tiles, index, 1, 0)


def on_device(stored, block_cols, out_cols):
    row, col = lax.axis_index("row"), lax.axis_index("col")
    core, high = col % 2, row % 2
    half = (row * COLS + col) // HOLDERS
    which = 2 * core + high
    spread = stored.reshape(DEVICES, PIECE, SIDE)
    held = lax.all_to_all(spread, AXES, split_axis=0, concat_axis=0, tiled=True)
    scalars = (
        block_cols.reshape(-1),
        out_cols.reshape(-1),
        jnp.stack([row, col]).astype(jnp.int32),
        jnp.asarray(copy_table(centre_copies))[which],
        jnp.asarray(copy_table(outer_copies))[which],
    )
    held, scalars = lax.optimization_barrier((held, scalars))
    cols, kept, place, centre, outer = scalars
    route = jnp.asarray(routes().reshape(2, -1))[half]
    outgoing = pick(route, held)
    received = lax.all_to_all(outgoing, AXES, split_axis=0, concat_axis=0, tiled=True)
    received = received.reshape(2, HOLDERS, PAIRS, PIECE, SIDE)

    def gathered(pieces, start, count):
        pieces = pieces[:, :, start : start + count].transpose(2, 0, 1, 3, 4)
        return pieces.reshape(-1, TILE, SIDE, SIDE)

    left = gathered(one(received, 1 - core), 0, 4)
    forward = moved(left[:3], lambda r, m, c: (r, m + 1 - 2 * c, c))
    backward = moved(left[1:], lambda r, m, c: (r, m - 1 + 2 * c, 1 - c))
    sibling = moved(left, lambda r, m, c: (r, m, 1 - c))
    mirror = gathered(one(received, core), 0, 4)
    own = gathered(received, 4, 2)
    sent = jnp.concatenate([one(own, 2 * (1 - high) + core), one(mirror, 2 - high)], 0)
    across = moved(sent, lambda r, m, c: (r ^ 1, m, c))
    kept_count = out_cols.shape[3]
    partial = products(
        cols,
        kept,
        place,
        centre,
        (own, mirror, left, sibling),
        copy_arrays(centre_copies),
        kept_count,
    )
    forward, backward, across, partial = lax.optimization_barrier(
        (forward, backward, across, partial)
    )
    shared = moved(
        jnp.concatenate([forward[:1], backward[2:]], 0), lambda r, m, c: (r, m, 1 - c)
    )
    return products(
        cols,
        kept,
        place,
        outer,
        (own, mirror, across, forward, backward, shared),
        copy_arrays(outer_copies),
        kept_count,
        partial,
    )


def solution(mesh):
    placed = (P("row", "col", None, None, None), P(), P("row", "col", None, None))
    return jax.shard_map(
        on_device,
        mesh=mesh,
        in_specs=placed,
        out_specs=P("row", "col", None, None, None, None),
        check_vma=False,
    )
```

```python
import functools

import jax
import jax.numpy as jnp
import numpy as np
from jax import lax
from jax.experimental import pallas as pl
from jax.experimental.pallas import tpu as pltpu
from jax.sharding import PartitionSpec as P

STEPS = 4
GRID = 16
ROWS = 8
COLS = 16
DEVICES = ROWS * COLS
AXES = ("row", "col")
TILE = 12
SIDE = 128
PIECE = 24
HOLDERS = 64

RIGHT_OWN, RIGHT_MIRROR, LEFT_OWN, LEFT_MIRROR = 0, 6, 12, 24
SLOTS = 36
CENTRE = (2, 3)
OUTER = (0, 1, 4, 5)


def slot_of(kind, rel, lead=0):
    return kind + (2 * rel + lead if kind in (LEFT_OWN, LEFT_MIRROR) else rel)


def centre_left(core):
    if core == 0:
        return ((LEFT_MIRROR, 3, 0), (LEFT_OWN, 3, 1), (LEFT_MIRROR, 3, 1), (LEFT_OWN, 2, 1))
    return ((LEFT_MIRROR, 2, 1), (LEFT_OWN, 2, 0), (LEFT_MIRROR, 2, 0), (LEFT_OWN, 3, 0))


def mirror_rels(core, high):
    return tuple(core + high + i for i in range(4))


def own_rels(core, high):
    rels = mirror_rels(core, high)
    return tuple(sorted(rels[:2], key=lambda rel: rel % 2)) + tuple(
        sorted(rels[2:], key=lambda rel: rel % 2)
    )


def shifted(tiles, by):
    return [(kind, rel + by, lead) for kind, rel, lead in tiles]


def from_neighbours(core):
    by = 2 * core * 2 - 2
    return shifted(centre_left(core)[:3], by), shifted(centre_left(1 - core)[1:], by)


def rights(array, kind, held, wanted):
    return [(array, held.index(rel), slot_of(kind, rel)) for rel in held if rel in wanted]


def centre_copies(core, high):
    copies = rights(0, RIGHT_OWN, own_rels(core, high), CENTRE)
    copies += rights(1, RIGHT_MIRROR, mirror_rels(core, high), CENTRE)
    copies += [(2, i, slot_of(*tile)) for i, tile in enumerate(centre_left(core))]
    copies += [(3, i, slot_of(*tile)) for i, tile in enumerate(centre_left(1 - core))]
    return copies


def outer_copies(core, high):
    copies = rights(0, RIGHT_OWN, own_rels(core, high), OUTER)
    copies += rights(1, RIGHT_MIRROR, mirror_rels(core, high), OUTER)
    missing = core if high else core + 4
    copies += [(2, 0, slot_of(RIGHT_OWN, missing)), (2, 1, slot_of(RIGHT_MIRROR, missing))]
    first, second = from_neighbours(core)
    copies += [(3, i, slot_of(*tile)) for i, tile in enumerate(first)]
    copies += [(4, i, slot_of(*tile)) for i, tile in enumerate(second)]
    first, second = from_neighbours(1 - core)
    copies += [(5, 0, slot_of(*first[0])), (5, 1, slot_of(*second[2]))]
    return copies


def copy_arrays(copies):
    return tuple(array for array, _, _ in copies(0, 0))


def copy_table(copies):
    table = []
    for core in (0, 1):
        for high in (0, 1):
            listed = copies(core, high)
            assert tuple(c[0] for c in listed) == copy_arrays(copies)
            table.append([c[1] for c in listed] + [c[2] for c in listed])
    return np.array(table, np.int32)


def source_of(tile, row, col):
    kind, rel, lead = tile
    ahead = (2 * row + 2 * (col // 2) + rel) % GRID
    own = 2 * row + lead
    lead, tail = {
        RIGHT_OWN: (ahead, col),
        RIGHT_MIRROR: (col, ahead),
        LEFT_OWN: (own, ahead),
        LEFT_MIRROR: (ahead, own),
    }[kind]
    return lead // 2 * COLS + tail, lead % 2


PAIRS = 6


def routes():
    table = np.zeros((2, DEVICES, PAIRS), np.int32)
    for device in range(DEVICES):
        row, col = divmod(device, COLS)
        core, high = col % 2, row % 2
        wanted = [[None] * PAIRS, [None] * PAIRS]
        for i in range(4):
            wanted[core][i] = (RIGHT_MIRROR, mirror_rels(core, high)[i], 0)
            wanted[1 - core][i] = centre_left(core)[i]
            wanted[i % 2][4 + i // 2] = (RIGHT_OWN, own_rels(core, high)[i], 0)
        for half in range(2):
            for pair in range(PAIRS):
                source, held = source_of(wanted[half][pair], row, col)
                assert held == half
                table[half, device, pair] = source
    return table


def pick_kernel(route_ref, held_ref, out_ref):
    group, pairs = out_ref.shape[:2]
    base = pl.program_id(0) * group * pairs

    def body(target, carry):
        for pair in range(pairs):
            out_ref[target, pair] = held_ref[route_ref[base + target * pairs + pair]]
        return carry

    lax.fori_loop(0, group, body, 0, unroll=4)


def pick(route, held):
    group = 16
    return pl.pallas_call(
        pick_kernel,
        grid_spec=pltpu.PrefetchScalarGridSpec(
            num_scalar_prefetch=1,
            grid=(DEVICES // group,),
            in_specs=[pl.BlockSpec((DEVICES, PIECE, SIDE), lambda t, *_: (0, 0, 0))],
            out_specs=pl.BlockSpec((group, PAIRS, PIECE, SIDE), lambda t, *_: (t, 0, 0, 0)),
        ),
        out_shape=jax.ShapeDtypeStruct((DEVICES, PAIRS, PIECE, SIDE), jnp.bfloat16),
        compiler_params=pltpu.CompilerParams(vmem_limit_bytes=16 << 20),
        cost_estimate=pl.CostEstimate(
            flops=0, bytes_accessed=2 * DEVICES * PAIRS * PIECE * SIDE * 2, transcendentals=0
        ),
    )(route, held)


def split_kernel(half_ref, received_ref, left_ref, forward_ref, backward_ref):
    count = left_ref.shape[0]
    for pair in range(count):
        pieces = received_ref[0, :, pair]
        left_ref[pair] = pieces
        if pair + 1 < count:
            forward_ref[pair] = pieces
        if pair:
            backward_ref[pair - 1] = pieces


def split(received, half, count):
    group = 16
    sizes = (count, count - 1, count - 1)
    results = pl.pallas_call(
        split_kernel,
        grid_spec=pltpu.PrefetchScalarGridSpec(
            num_scalar_prefetch=1,
            grid=(HOLDERS // group,),
            in_specs=[
                pl.BlockSpec(
                    (1, group, count, PIECE, SIDE), lambda t, half: (half[0], t, 0, 0, 0)
                )
            ],
            out_specs=[
                pl.BlockSpec((size, group, PIECE, SIDE), lambda t, half: (0, t, 0, 0))
                for size in sizes
            ],
        ),
        out_shape=[
            jax.ShapeDtypeStruct((size, HOLDERS, PIECE, SIDE), received.dtype) for size in sizes
        ],
        compiler_params=pltpu.CompilerParams(vmem_limit_bytes=16 << 20),
        cost_estimate=pl.CostEstimate(flops=0, bytes_accessed=6 << 20, transcendentals=0),
    )(half.reshape(1), received)
    return [array.reshape(-1, TILE, SIDE, SIDE) for array in results]


def matmul(left, right, right_dim):
    return lax.dot_general(
        left, right, (((1,), (right_dim,)), ((), ())), preferred_element_type=jnp.float32
    )


def product_kernel(sources, from_arrays, last, cols_ref, kept_ref, place_ref, copy_ref, *refs):
    arrays, refs = refs[:sources], refs[sources:]
    if last:
        partial_ref, refs = refs[0], refs[1:]
    out_ref, tiles, total, right_inv, left_inv, sems = refs
    lines, kept_count = out_ref.shape[2:4]
    step = pl.program_id(0)
    slot = step * lines // TILE
    row, col = place_ref[0], place_ref[1]
    core = col % 2
    first = 2 * row + col - core

    def group(rel):
        return (first + rel) % GRID

    def entry(lead, tail, line):
        return cols_ref[(lead * GRID + tail) * TILE + line]

    @pl.when(step == 0)
    def _():
        count = len(from_arrays)
        started = [
            pltpu.make_async_copy(
                arrays[array].at[copy_ref[index]],
                tiles.at[copy_ref[count + index]],
                sems.at[index],
            )
            for index, array in enumerate(from_arrays)
        ]
        for copy in started:
            copy.start()
        for rel in OUTER if last else CENTRE:
            ahead = group(rel)
            for q in range(TILE):
                right_inv[rel * TILE + entry(col, ahead, q)] = q
                for half in range(2):
                    left_inv[(2 * rel + half) * TILE + entry(ahead, 2 * row + half, q)] = q
        for copy in started:
            copy.wait()

    total[...] = jnp.zeros_like(total)
    if last:
        edge = slot + core
        rels = (jnp.where(edge == 2, 4, edge), jnp.where(edge == 0, 1, 3 + edge))
    else:
        rels = CENTRE
    for sub in range(lines):
        line = step * lines % TILE + sub
        for rel in rels:
            ahead = group(rel)
            own_col = entry(2 * row + slot, ahead, line)
            mirror_col = left_inv[(2 * rel + slot) * TILE + line]
            own = tiles[LEFT_OWN + 2 * rel + slot, line]
            mirror = tiles[LEFT_MIRROR + 2 * rel + slot, mirror_col].T
            for left, middle in ((own, own_col), (mirror, mirror_col)):
                flipped = right_inv[rel * TILE + middle]
                total[sub, entry(ahead, col, middle)] += matmul(
                    left, tiles[RIGHT_OWN + rel, middle], 0
                )
                total[sub, flipped] += matmul(left, tiles[RIGHT_MIRROR + rel, flipped], 1)
    for sub in range(lines):
        for o in range(kept_count):
            value = total[sub, kept_ref[(step * lines + sub) * kept_count + o]]
            if last:
                value = value + partial_ref[0, 0, sub, o]
            out_ref[0, 0, sub, o] = value.astype(out_ref.dtype)


def products(cols, kept, place, table, arrays, from_arrays, kept_count, partial=None):
    last = partial is not None
    lines = 2
    block = pl.BlockSpec(
        (1, 1, lines, kept_count, SIDE, SIDE),
        lambda t, *_: (t * lines // TILE, 0, t % (TILE // lines), 0, 0, 0),
    )
    dtype = jnp.bfloat16 if last else jnp.float32
    operands = list(arrays) + ([partial] if last else [])
    return pl.pallas_call(
        functools.partial(product_kernel, len(arrays), from_arrays, last),
        grid_spec=pltpu.PrefetchScalarGridSpec(
            num_scalar_prefetch=4,
            grid=(2 * TILE // lines,),
            in_specs=[pl.BlockSpec(memory_space=pl.ANY)] * len(arrays) + [block] * last,
            out_specs=block,
            scratch_shapes=[
                pltpu.VMEM((SLOTS, TILE, SIDE, SIDE), jnp.bfloat16),
                pltpu.VMEM((lines, TILE, SIDE, SIDE), jnp.float32),
                pltpu.SMEM((6 * TILE,), jnp.int32),
                pltpu.SMEM((12 * TILE,), jnp.int32),
                pltpu.SemaphoreType.DMA((len(from_arrays),)),
            ],
        ),
        out_shape=jax.ShapeDtypeStruct((2, 1, TILE, kept_count, SIDE, SIDE), dtype),
        compiler_params=pltpu.CompilerParams(vmem_limit_bytes=30 << 20),
        cost_estimate=pl.CostEstimate(
            flops=192 * 2 * SIDE**3, bytes_accessed=25 << 20, transcendentals=0
        ),
    )(cols, kept, place, table, *operands)


def moved(tiles, target):
    pairs = []
    for row in range(ROWS):
        for col in range(COLS):
            to_row, to_chip, to_core = target(row, col // 2, col % 2)
            to = to_row % ROWS * COLS + 2 * (to_chip % (COLS // 2)) + to_core
            pairs.append((row * COLS + col, to))
    return lax.ppermute(tiles, AXES, pairs)


def one(tiles, index):
    return lax.dynamic_slice_in_dim(tiles, index, 1, 0)


def on_device(stored, block_cols, out_cols):
    row, col = lax.axis_index("row"), lax.axis_index("col")
    core, high = col % 2, row % 2
    half = (row * COLS + col) // HOLDERS
    which = 2 * core + high
    spread = stored.reshape(DEVICES, PIECE, SIDE)
    held = lax.all_to_all(spread, AXES, split_axis=0, concat_axis=0, tiled=True)
    scalars = (
        block_cols.reshape(-1),
        out_cols.reshape(-1),
        jnp.stack([row, col]).astype(jnp.int32),
        jnp.asarray(copy_table(centre_copies))[which],
        jnp.asarray(copy_table(outer_copies))[which],
    )
    held, scalars = lax.optimization_barrier((held, scalars))
    cols, kept, place, centre, outer = scalars
    route = jnp.asarray(routes().reshape(2, -1))[half]
    outgoing = pick(route, held)
    received = lax.all_to_all(outgoing, AXES, split_axis=0, concat_axis=0, tiled=True)
    received = received.reshape(2, HOLDERS, PAIRS, PIECE, SIDE)

    def gathered(pieces, start, count):
        pieces = pieces[:, :, start : start + count].transpose(2, 0, 1, 3, 4)
        return pieces.reshape(-1, TILE, SIDE, SIDE)

    left, forward, backward = split(received, 1 - core, 4)
    forward = moved(forward, lambda r, m, c: (r, m + 1 - 2 * c, c))
    backward = moved(backward, lambda r, m, c: (r, m - 1 + 2 * c, 1 - c))
    sibling = moved(left, lambda r, m, c: (r, m, 1 - c))
    mirror = gathered(one(received, core), 0, 4)
    own = gathered(received, 4, 2)
    sent = jnp.concatenate([one(own, 2 * (1 - high) + core), one(mirror, 2 - high)], 0)
    across = moved(sent, lambda r, m, c: (r ^ 1, m, c))
    kept_count = out_cols.shape[3]
    partial = products(
        cols,
        kept,
        place,
        centre,
        (own, mirror, left, sibling),
        copy_arrays(centre_copies),
        kept_count,
    )
    forward, backward, across, partial = lax.optimization_barrier(
        (forward, backward, across, partial)
    )
    shared = moved(
        jnp.concatenate([forward[:1], backward[2:]], 0), lambda r, m, c: (r, m, 1 - c)
    )
    return products(
        cols,
        kept,
        place,
        outer,
        (own, mirror, across, forward, backward, shared),
        copy_arrays(outer_copies),
        kept_count,
        partial,
    )


def solution(mesh):
    placed = (P("row", "col", None, None, None), P(), P("row", "col", None, None))
    return jax.shard_map(
        on_device,
        mesh=mesh,
        in_specs=placed,
        out_specs=P("row", "col", None, None, None, None),
        check_vma=False,
    )
```

```python
import functools

import jax
import jax.numpy as jnp
import numpy as np
from jax import lax
from jax.experimental import pallas as pl
from jax.experimental.pallas import tpu as pltpu
from jax.sharding import PartitionSpec as P

STEPS = 4
GRID = 16
ROWS = 8
COLS = 16
DEVICES = ROWS * COLS
AXES = ("row", "col")
TILE = 12
SIDE = 128
PIECE = 24
HOLDERS = 64

RIGHT_OWN, RIGHT_MIRROR, LEFT_OWN, LEFT_MIRROR = 0, 6, 12, 24
SLOTS = 36
CENTRE = (2, 3)
OUTER = (0, 1, 4, 5)


def slot_of(kind, rel, lead=0):
    return kind + (2 * rel + lead if kind in (LEFT_OWN, LEFT_MIRROR) else rel)


def centre_left(core):
    if core == 0:
        return ((LEFT_MIRROR, 3, 0), (LEFT_OWN, 3, 1), (LEFT_MIRROR, 3, 1), (LEFT_OWN, 2, 1))
    return ((LEFT_MIRROR, 2, 1), (LEFT_OWN, 2, 0), (LEFT_MIRROR, 2, 0), (LEFT_OWN, 3, 0))


def mirror_rels(core, high):
    return tuple(core + high + i for i in range(4))


def own_rels(core, high):
    rels = mirror_rels(core, high)
    return tuple(sorted(rels[:2], key=lambda rel: rel % 2)) + tuple(
        sorted(rels[2:], key=lambda rel: rel % 2)
    )


def shifted(tiles, by):
    return [(kind, rel + by, lead) for kind, rel, lead in tiles]


def from_neighbours(core):
    by = 2 * core * 2 - 2
    return shifted(centre_left(core)[:3], by), shifted(centre_left(1 - core)[1:], by)


def rights(array, kind, held, wanted):
    return [(array, held.index(rel), slot_of(kind, rel)) for rel in held if rel in wanted]


def centre_copies(core, high):
    copies = rights(0, RIGHT_OWN, own_rels(core, high), CENTRE)
    copies += rights(1, RIGHT_MIRROR, mirror_rels(core, high), CENTRE)
    copies += [(2, i, slot_of(*tile)) for i, tile in enumerate(centre_left(core))]
    copies += [(3, i, slot_of(*tile)) for i, tile in enumerate(centre_left(1 - core))]
    return copies


def outer_copies(core, high):
    copies = rights(0, RIGHT_OWN, own_rels(core, high), OUTER)
    copies += rights(1, RIGHT_MIRROR, mirror_rels(core, high), OUTER)
    missing = core if high else core + 4
    copies += [(2, 0, slot_of(RIGHT_OWN, missing)), (2, 1, slot_of(RIGHT_MIRROR, missing))]
    first, second = from_neighbours(core)
    copies += [(3, 0, slot_of(*first[0])), (4, 0, slot_of(*second[2]))]
    copies += [(5, i, slot_of(*tile)) for i, tile in enumerate(first[1:])]
    copies += [(6, i, slot_of(*tile)) for i, tile in enumerate(second[:2])]
    first, second = from_neighbours(1 - core)
    copies += [(7, 0, slot_of(*first[0])), (7, 1, slot_of(*second[2]))]
    return copies


def copy_arrays(copies):
    return tuple(array for array, _, _ in copies(0, 0))


def copy_table(copies):
    table = []
    for core in (0, 1):
        for high in (0, 1):
            listed = copies(core, high)
            assert tuple(c[0] for c in listed) == copy_arrays(copies)
            table.append([c[1] for c in listed] + [c[2] for c in listed])
    return np.array(table, np.int32)


def source_of(tile, row, col):
    kind, rel, lead = tile
    ahead = (2 * row + 2 * (col // 2) + rel) % GRID
    own = 2 * row + lead
    lead, tail = {
        RIGHT_OWN: (ahead, col),
        RIGHT_MIRROR: (col, ahead),
        LEFT_OWN: (own, ahead),
        LEFT_MIRROR: (ahead, own),
    }[kind]
    return lead // 2 * COLS + tail, lead % 2


PAIRS = 6


def routes():
    table = np.zeros((2, DEVICES, PAIRS), np.int32)
    for device in range(DEVICES):
        row, col = divmod(device, COLS)
        core, high = col % 2, row % 2
        wanted = [[None] * PAIRS, [None] * PAIRS]
        for i in range(4):
            wanted[core][i] = (RIGHT_MIRROR, mirror_rels(core, high)[i], 0)
            wanted[1 - core][i] = centre_left(core)[i]
            wanted[i % 2][4 + i // 2] = (RIGHT_OWN, own_rels(core, high)[i], 0)
        for half in range(2):
            for pair in range(PAIRS):
                source, held = source_of(wanted[half][pair], row, col)
                assert held == half
                table[half, device, pair] = source
    return table


def pick_kernel(route_ref, held_ref, out_ref):
    group, pairs = out_ref.shape[:2]
    base = pl.program_id(0) * group * pairs

    def body(target, carry):
        for pair in range(pairs):
            out_ref[target, pair] = held_ref[route_ref[base + target * pairs + pair]]
        return carry

    lax.fori_loop(0, group, body, 0, unroll=4)


def pick(route, held):
    group = 16
    return pl.pallas_call(
        pick_kernel,
        grid_spec=pltpu.PrefetchScalarGridSpec(
            num_scalar_prefetch=1,
            grid=(DEVICES // group,),
            in_specs=[pl.BlockSpec((DEVICES, PIECE, SIDE), lambda t, *_: (0, 0, 0))],
            out_specs=pl.BlockSpec((group, PAIRS, PIECE, SIDE), lambda t, *_: (t, 0, 0, 0)),
        ),
        out_shape=jax.ShapeDtypeStruct((DEVICES, PAIRS, PIECE, SIDE), jnp.bfloat16),
        compiler_params=pltpu.CompilerParams(vmem_limit_bytes=16 << 20),
        cost_estimate=pl.CostEstimate(
            flops=0, bytes_accessed=2 * DEVICES * PAIRS * PIECE * SIDE * 2, transcendentals=0
        ),
    )(route, held)


def split_kernel(half_ref, received_ref, left_ref, head_ref, middle_ref, tail_ref):
    for pair in range(4):
        left_ref[pair] = received_ref[0, :, pair]
    head_ref[0] = received_ref[0, :, 0]
    middle_ref[0] = received_ref[0, :, 1]
    middle_ref[1] = received_ref[0, :, 2]
    tail_ref[0] = received_ref[0, :, 3]


def split(received, half):
    group = 16
    sizes = (4, 1, 2, 1)
    results = pl.pallas_call(
        split_kernel,
        grid_spec=pltpu.PrefetchScalarGridSpec(
            num_scalar_prefetch=1,
            grid=(HOLDERS // group,),
            in_specs=[
                pl.BlockSpec((1, group, 4, PIECE, SIDE), lambda t, half: (half[0], t, 0, 0, 0))
            ],
            out_specs=[
                pl.BlockSpec((size, group, PIECE, SIDE), lambda t, half: (0, t, 0, 0))
                for size in sizes
            ],
        ),
        out_shape=[
            jax.ShapeDtypeStruct((size, HOLDERS, PIECE, SIDE), received.dtype) for size in sizes
        ],
        compiler_params=pltpu.CompilerParams(vmem_limit_bytes=16 << 20),
        cost_estimate=pl.CostEstimate(flops=0, bytes_accessed=5 << 20, transcendentals=0),
    )(half.reshape(1), received)
    return [array.reshape(-1, TILE, SIDE, SIDE) for array in results]


def matmul(left, right, right_dim):
    return lax.dot_general(
        left, right, (((1,), (right_dim,)), ((), ())), preferred_element_type=jnp.float32
    )


def product_kernel(sources, from_arrays, last, cols_ref, kept_ref, place_ref, copy_ref, *refs):
    arrays, refs = refs[:sources], refs[sources:]
    if last:
        partial_ref, refs = refs[0], refs[1:]
    out_ref, tiles, total, right_inv, left_inv, sems = refs
    lines, kept_count = out_ref.shape[2:4]
    step = pl.program_id(0)
    slot = step * lines // TILE
    row, col = place_ref[0], place_ref[1]
    core = col % 2
    first = 2 * row + col - core

    def group(rel):
        return (first + rel) % GRID

    def entry(lead, tail, line):
        return cols_ref[(lead * GRID + tail) * TILE + line]

    @pl.when(step == 0)
    def _():
        count = len(from_arrays)
        started = [
            pltpu.make_async_copy(
                arrays[array].at[copy_ref[index]],
                tiles.at[copy_ref[count + index]],
                sems.at[index],
            )
            for index, array in enumerate(from_arrays)
        ]
        for copy in started:
            copy.start()
        for rel in OUTER if last else CENTRE:
            ahead = group(rel)
            for q in range(TILE):
                right_inv[rel * TILE + entry(col, ahead, q)] = q
                for half in range(2):
                    left_inv[(2 * rel + half) * TILE + entry(ahead, 2 * row + half, q)] = q
        for copy in started:
            copy.wait()

    total[...] = jnp.zeros_like(total)
    if last:
        edge = slot + core
        rels = (jnp.where(edge == 2, 4, edge), jnp.where(edge == 0, 1, 3 + edge))
    else:
        rels = CENTRE
    for sub in range(lines):
        line = step * lines % TILE + sub
        for rel in rels:
            ahead = group(rel)
            own_col = entry(2 * row + slot, ahead, line)
            mirror_col = left_inv[(2 * rel + slot) * TILE + line]
            own = tiles[LEFT_OWN + 2 * rel + slot, line]
            mirror = tiles[LEFT_MIRROR + 2 * rel + slot, mirror_col].T
            for left, middle in ((own, own_col), (mirror, mirror_col)):
                flipped = right_inv[rel * TILE + middle]
                total[sub, entry(ahead, col, middle)] += matmul(
                    left, tiles[RIGHT_OWN + rel, middle], 0
                )
                total[sub, flipped] += matmul(left, tiles[RIGHT_MIRROR + rel, flipped], 1)
    for sub in range(lines):
        for o in range(kept_count):
            value = total[sub, kept_ref[(step * lines + sub) * kept_count + o]]
            if last:
                value = value + partial_ref[0, 0, sub, o]
            out_ref[0, 0, sub, o] = value.astype(out_ref.dtype)


def products(cols, kept, place, table, arrays, from_arrays, kept_count, partial=None):
    last = partial is not None
    lines = 2
    block = pl.BlockSpec(
        (1, 1, lines, kept_count, SIDE, SIDE),
        lambda t, *_: (t * lines // TILE, 0, t % (TILE // lines), 0, 0, 0),
    )
    dtype = jnp.bfloat16 if last else jnp.float32
    operands = list(arrays) + ([partial] if last else [])
    return pl.pallas_call(
        functools.partial(product_kernel, len(arrays), from_arrays, last),
        grid_spec=pltpu.PrefetchScalarGridSpec(
            num_scalar_prefetch=4,
            grid=(2 * TILE // lines,),
            in_specs=[pl.BlockSpec(memory_space=pl.ANY)] * len(arrays) + [block] * last,
            out_specs=block,
            scratch_shapes=[
                pltpu.VMEM((SLOTS, TILE, SIDE, SIDE), jnp.bfloat16),
                pltpu.VMEM((lines, TILE, SIDE, SIDE), jnp.float32),
                pltpu.SMEM((6 * TILE,), jnp.int32),
                pltpu.SMEM((12 * TILE,), jnp.int32),
                pltpu.SemaphoreType.DMA((len(from_arrays),)),
            ],
        ),
        out_shape=jax.ShapeDtypeStruct((2, 1, TILE, kept_count, SIDE, SIDE), dtype),
        compiler_params=pltpu.CompilerParams(vmem_limit_bytes=30 << 20),
        cost_estimate=pl.CostEstimate(
            flops=192 * 2 * SIDE**3, bytes_accessed=25 << 20, transcendentals=0
        ),
    )(cols, kept, place, table, *operands)


def moved(tiles, target):
    pairs = []
    for row in range(ROWS):
        for col in range(COLS):
            to_row, to_chip, to_core = target(row, col // 2, col % 2)
            to = to_row % ROWS * COLS + 2 * (to_chip % (COLS // 2)) + to_core
            pairs.append((row * COLS + col, to))
    return lax.ppermute(tiles, AXES, pairs)


def one(tiles, index):
    return lax.dynamic_slice_in_dim(tiles, index, 1, 0)


def on_device(stored, block_cols, out_cols):
    row, col = lax.axis_index("row"), lax.axis_index("col")
    core, high = col % 2, row % 2
    half = (row * COLS + col) // HOLDERS
    which = 2 * core + high
    spread = stored.reshape(DEVICES, PIECE, SIDE)
    held = lax.all_to_all(spread, AXES, split_axis=0, concat_axis=0, tiled=True)
    scalars = (
        block_cols.reshape(-1),
        out_cols.reshape(-1),
        jnp.stack([row, col]).astype(jnp.int32),
        jnp.asarray(copy_table(centre_copies))[which],
        jnp.asarray(copy_table(outer_copies))[which],
    )
    held, scalars = lax.optimization_barrier((held, scalars))
    cols, kept, place, centre, outer = scalars
    route = jnp.asarray(routes().reshape(2, -1))[half]
    outgoing = pick(route, held)
    received = lax.all_to_all(outgoing, AXES, split_axis=0, concat_axis=0, tiled=True)
    received = received.reshape(2, HOLDERS, PAIRS, PIECE, SIDE)

    def gathered(pieces, start, count):
        pieces = pieces[:, :, start : start + count].transpose(2, 0, 1, 3, 4)
        return pieces.reshape(-1, TILE, SIDE, SIDE)

    left, head, middle, tail = split(received, 1 - core)

    def forward(tiles):
        return moved(tiles, lambda r, m, c: (r, m + 1 - 2 * c, c))

    def backward(tiles):
        return moved(tiles, lambda r, m, c: (r, m - 1 + 2 * c, 1 - c))

    head, tail = forward(head), backward(tail)
    ahead, behind = forward(middle), backward(middle)
    sibling = moved(left, lambda r, m, c: (r, m, 1 - c))
    mirror = gathered(one(received, core), 0, 4)
    own = gathered(received, 4, 2)
    sent = jnp.concatenate([one(own, 2 * (1 - high) + core), one(mirror, 2 - high)], 0)
    across = moved(sent, lambda r, m, c: (r ^ 1, m, c))
    kept_count = out_cols.shape[3]
    partial = products(
        cols,
        kept,
        place,
        centre,
        (own, mirror, left, sibling),
        copy_arrays(centre_copies),
        kept_count,
    )
    head, tail, partial = lax.optimization_barrier((head, tail, partial))
    shared = moved(jnp.concatenate([head, tail], 0), lambda r, m, c: (r, m, 1 - c))
    return products(
        cols,
        kept,
        place,
        outer,
        (own, mirror, across, head, tail, ahead, behind, shared),
        copy_arrays(outer_copies),
        kept_count,
        partial,
    )


def solution(mesh):
    placed = (P("row", "col", None, None, None), P(), P("row", "col", None, None))
    return jax.shard_map(
        on_device,
        mesh=mesh,
        in_specs=placed,
        out_specs=P("row", "col", None, None, None, None),
        check_vma=False,
    )
```

```python
import functools

import jax
import jax.numpy as jnp
import numpy as np
from jax import lax
from jax.experimental import pallas as pl
from jax.experimental.pallas import tpu as pltpu
from jax.sharding import PartitionSpec as P

STEPS = 4
GRID = 16
ROWS = 8
COLS = 16
DEVICES = ROWS * COLS
AXES = ("row", "col")
TILE = 12
SIDE = 128
PIECE = 24
HOLDERS = 64

RIGHT_OWN, RIGHT_MIRROR, LEFT_OWN, LEFT_MIRROR = 0, 6, 12, 24
SLOTS = 36
CENTRE = (2, 3)
OUTER = (0, 1, 4, 5)


def slot_of(kind, rel, lead=0):
    return kind + (2 * rel + lead if kind in (LEFT_OWN, LEFT_MIRROR) else rel)


def centre_left(core):
    if core == 0:
        return ((LEFT_MIRROR, 3, 0), (LEFT_OWN, 3, 1), (LEFT_MIRROR, 3, 1), (LEFT_OWN, 2, 1))
    return ((LEFT_MIRROR, 2, 1), (LEFT_OWN, 2, 0), (LEFT_MIRROR, 2, 0), (LEFT_OWN, 3, 0))


def mirror_rels(core, high):
    return tuple(core + high + i for i in range(4))


def own_rels(core, high):
    rels = mirror_rels(core, high)
    return tuple(sorted(rels[:2], key=lambda rel: rel % 2)) + tuple(
        sorted(rels[2:], key=lambda rel: rel % 2)
    )


def shifted(tiles, by):
    return [(kind, rel + by, lead) for kind, rel, lead in tiles]


def from_neighbours(core):
    by = 2 * core * 2 - 2
    return shifted(centre_left(core)[:3], by), shifted(centre_left(1 - core)[1:], by)


def rights(array, kind, held, wanted):
    return [(array, held.index(rel), slot_of(kind, rel)) for rel in held if rel in wanted]


def centre_copies(core, high):
    copies = rights(0, RIGHT_OWN, own_rels(core, high), CENTRE)
    copies += rights(1, RIGHT_MIRROR, mirror_rels(core, high), CENTRE)
    copies += [(2, i, slot_of(*tile)) for i, tile in enumerate(centre_left(core))]
    copies += [(3, i, slot_of(*tile)) for i, tile in enumerate(centre_left(1 - core))]
    return copies


def outer_copies(core, high):
    copies = rights(0, RIGHT_OWN, own_rels(core, high), OUTER)
    copies += rights(1, RIGHT_MIRROR, mirror_rels(core, high), OUTER)
    missing = core if high else core + 4
    copies += [(2, 0, slot_of(RIGHT_OWN, missing)), (2, 1, slot_of(RIGHT_MIRROR, missing))]
    first, second = from_neighbours(core)
    copies += [(3, 0, slot_of(*first[0])), (4, 0, slot_of(*second[2]))]
    copies += [(5, i, slot_of(*tile)) for i, tile in enumerate(first[1:])]
    copies += [(6, i, slot_of(*tile)) for i, tile in enumerate(second[:2])]
    first, second = from_neighbours(1 - core)
    copies += [(7, 0, slot_of(*first[0])), (7, 1, slot_of(*second[2]))]
    return copies


def copy_arrays(copies):
    return tuple(array for array, _, _ in copies(0, 0))


def copy_table(copies):
    table = []
    for core in (0, 1):
        for high in (0, 1):
            listed = copies(core, high)
            assert tuple(c[0] for c in listed) == copy_arrays(copies)
            table.append([c[1] for c in listed] + [c[2] for c in listed])
    return np.array(table, np.int32)


def source_of(tile, row, col):
    kind, rel, lead = tile
    ahead = (2 * row + 2 * (col // 2) + rel) % GRID
    own = 2 * row + lead
    lead, tail = {
        RIGHT_OWN: (ahead, col),
        RIGHT_MIRROR: (col, ahead),
        LEFT_OWN: (own, ahead),
        LEFT_MIRROR: (ahead, own),
    }[kind]
    return lead // 2 * COLS + tail, lead % 2


PAIRS = 6


def routes():
    table = np.zeros((2, DEVICES, PAIRS), np.int32)
    for device in range(DEVICES):
        row, col = divmod(device, COLS)
        core, high = col % 2, row % 2
        wanted = [[None] * PAIRS, [None] * PAIRS]
        for i in range(4):
            wanted[core][i] = (RIGHT_MIRROR, mirror_rels(core, high)[i], 0)
            wanted[1 - core][i] = centre_left(core)[i]
            wanted[i % 2][4 + i // 2] = (RIGHT_OWN, own_rels(core, high)[i], 0)
        for half in range(2):
            for pair in range(PAIRS):
                source, held = source_of(wanted[half][pair], row, col)
                assert held == half
                table[half, device, pair] = source
    return table


def pick_kernel(route_ref, held_ref, out_ref):
    group, pairs = out_ref.shape[:2]
    base = pl.program_id(0) * group * pairs

    def body(target, carry):
        for pair in range(pairs):
            out_ref[target, pair] = held_ref[route_ref[base + target * pairs + pair]]
        return carry

    lax.fori_loop(0, group, body, 0, unroll=4)


def pick(route, held):
    group = 32
    return pl.pallas_call(
        pick_kernel,
        grid_spec=pltpu.PrefetchScalarGridSpec(
            num_scalar_prefetch=1,
            grid=(DEVICES // group,),
            in_specs=[pl.BlockSpec((DEVICES, PIECE, SIDE), lambda t, *_: (0, 0, 0))],
            out_specs=pl.BlockSpec((group, PAIRS, PIECE, SIDE), lambda t, *_: (t, 0, 0, 0)),
        ),
        out_shape=jax.ShapeDtypeStruct((DEVICES, PAIRS, PIECE, SIDE), jnp.bfloat16),
        compiler_params=pltpu.CompilerParams(vmem_limit_bytes=16 << 20),
        cost_estimate=pl.CostEstimate(
            flops=0, bytes_accessed=2 * DEVICES * PAIRS * PIECE * SIDE * 2, transcendentals=0
        ),
    )(route, held)


def split_kernel(half_ref, received_ref, left_ref, head_ref, middle_ref, tail_ref):
    for pair in range(4):
        left_ref[pair] = received_ref[0, :, pair]
    head_ref[0] = received_ref[0, :, 0]
    middle_ref[0] = received_ref[0, :, 1]
    middle_ref[1] = received_ref[0, :, 2]
    tail_ref[0] = received_ref[0, :, 3]


def split(received, half):
    group = 32
    sizes = (4, 1, 2, 1)
    results = pl.pallas_call(
        split_kernel,
        grid_spec=pltpu.PrefetchScalarGridSpec(
            num_scalar_prefetch=1,
            grid=(HOLDERS // group,),
            in_specs=[
                pl.BlockSpec((1, group, 4, PIECE, SIDE), lambda t, half: (half[0], t, 0, 0, 0))
            ],
            out_specs=[
                pl.BlockSpec((size, group, PIECE, SIDE), lambda t, half: (0, t, 0, 0))
                for size in sizes
            ],
        ),
        out_shape=[
            jax.ShapeDtypeStruct((size, HOLDERS, PIECE, SIDE), received.dtype) for size in sizes
        ],
        compiler_params=pltpu.CompilerParams(vmem_limit_bytes=16 << 20),
        cost_estimate=pl.CostEstimate(flops=0, bytes_accessed=5 << 20, transcendentals=0),
    )(half.reshape(1), received)
    return [array.reshape(-1, TILE, SIDE, SIDE) for array in results]


def matmul(left, right, right_dim):
    return lax.dot_general(
        left, right, (((1,), (right_dim,)), ((), ())), preferred_element_type=jnp.float32
    )


def product_kernel(sources, from_arrays, last, cols_ref, kept_ref, place_ref, copy_ref, *refs):
    arrays, refs = refs[:sources], refs[sources:]
    if last:
        partial_ref, refs = refs[0], refs[1:]
    out_ref, tiles, total, right_inv, left_inv, sems = refs
    lines, kept_count = out_ref.shape[2:4]
    step = pl.program_id(0)
    slot = step * lines // TILE
    row, col = place_ref[0], place_ref[1]
    core = col % 2
    first = 2 * row + col - core

    def group(rel):
        return (first + rel) % GRID

    def entry(lead, tail, line):
        return cols_ref[(lead * GRID + tail) * TILE + line]

    @pl.when(step == 0)
    def _():
        count = len(from_arrays)
        started = [
            pltpu.make_async_copy(
                arrays[array].at[copy_ref[index]],
                tiles.at[copy_ref[count + index]],
                sems.at[index],
            )
            for index, array in enumerate(from_arrays)
        ]
        for copy in started:
            copy.start()
        for rel in OUTER if last else CENTRE:
            ahead = group(rel)
            for q in range(TILE):
                right_inv[rel * TILE + entry(col, ahead, q)] = q
                for half in range(2):
                    left_inv[(2 * rel + half) * TILE + entry(ahead, 2 * row + half, q)] = q
        for copy in started:
            copy.wait()

    total[...] = jnp.zeros_like(total)
    if last:
        edge = slot + core
        rels = (jnp.where(edge == 2, 4, edge), jnp.where(edge == 0, 1, 3 + edge))
    else:
        rels = CENTRE
    for sub in range(lines):
        line = step * lines % TILE + sub
        for rel in rels:
            ahead = group(rel)
            own_col = entry(2 * row + slot, ahead, line)
            mirror_col = left_inv[(2 * rel + slot) * TILE + line]
            own = tiles[LEFT_OWN + 2 * rel + slot, line]
            mirror = tiles[LEFT_MIRROR + 2 * rel + slot, mirror_col].T
            for left, middle in ((own, own_col), (mirror, mirror_col)):
                flipped = right_inv[rel * TILE + middle]
                total[sub, entry(ahead, col, middle)] += matmul(
                    left, tiles[RIGHT_OWN + rel, middle], 0
                )
                total[sub, flipped] += matmul(left, tiles[RIGHT_MIRROR + rel, flipped], 1)
    for sub in range(lines):
        for o in range(kept_count):
            value = total[sub, kept_ref[(step * lines + sub) * kept_count + o]]
            if last:
                value = value + partial_ref[0, 0, sub, o]
            out_ref[0, 0, sub, o] = value.astype(out_ref.dtype)


def products(cols, kept, place, table, arrays, from_arrays, kept_count, partial=None):
    last = partial is not None
    lines = 2
    block = pl.BlockSpec(
        (1, 1, lines, kept_count, SIDE, SIDE),
        lambda t, *_: (t * lines // TILE, 0, t % (TILE // lines), 0, 0, 0),
    )
    dtype = jnp.bfloat16 if last else jnp.float32
    operands = list(arrays) + ([partial] if last else [])
    return pl.pallas_call(
        functools.partial(product_kernel, len(arrays), from_arrays, last),
        grid_spec=pltpu.PrefetchScalarGridSpec(
            num_scalar_prefetch=4,
            grid=(2 * TILE // lines,),
            in_specs=[pl.BlockSpec(memory_space=pl.ANY)] * len(arrays) + [block] * last,
            out_specs=block,
            scratch_shapes=[
                pltpu.VMEM((SLOTS, TILE, SIDE, SIDE), jnp.bfloat16),
                pltpu.VMEM((lines, TILE, SIDE, SIDE), jnp.float32),
                pltpu.SMEM((6 * TILE,), jnp.int32),
                pltpu.SMEM((12 * TILE,), jnp.int32),
                pltpu.SemaphoreType.DMA((len(from_arrays),)),
            ],
        ),
        out_shape=jax.ShapeDtypeStruct((2, 1, TILE, kept_count, SIDE, SIDE), dtype),
        compiler_params=pltpu.CompilerParams(vmem_limit_bytes=30 << 20),
        cost_estimate=pl.CostEstimate(
            flops=192 * 2 * SIDE**3, bytes_accessed=25 << 20, transcendentals=0
        ),
    )(cols, kept, place, table, *operands)


def moved(tiles, target):
    pairs = []
    for row in range(ROWS):
        for col in range(COLS):
            to_row, to_chip, to_core = target(row, col // 2, col % 2)
            to = to_row % ROWS * COLS + 2 * (to_chip % (COLS // 2)) + to_core
            pairs.append((row * COLS + col, to))
    return lax.ppermute(tiles, AXES, pairs)


def one(tiles, index):
    return lax.dynamic_slice_in_dim(tiles, index, 1, 0)


def on_device(stored, block_cols, out_cols):
    row, col = lax.axis_index("row"), lax.axis_index("col")
    core, high = col % 2, row % 2
    half = (row * COLS + col) // HOLDERS
    which = 2 * core + high
    spread = stored.reshape(DEVICES, PIECE, SIDE)
    held = lax.all_to_all(spread, AXES, split_axis=0, concat_axis=0, tiled=True)
    scalars = (
        block_cols.reshape(-1),
        out_cols.reshape(-1),
        jnp.stack([row, col]).astype(jnp.int32),
        jnp.asarray(copy_table(centre_copies))[which],
        jnp.asarray(copy_table(outer_copies))[which],
    )
    held, scalars = lax.optimization_barrier((held, scalars))
    cols, kept, place, centre, outer = scalars
    route = jnp.asarray(routes().reshape(2, -1))[half]
    outgoing = pick(route, held)
    received = lax.all_to_all(outgoing, AXES, split_axis=0, concat_axis=0, tiled=True)
    received = received.reshape(2, HOLDERS, PAIRS, PIECE, SIDE)

    def gathered(pieces, start, count):
        pieces = pieces[:, :, start : start + count].transpose(2, 0, 1, 3, 4)
        return pieces.reshape(-1, TILE, SIDE, SIDE)

    left, head, middle, tail = split(received, 1 - core)

    def forward(tiles):
        return moved(tiles, lambda r, m, c: (r, m + 1 - 2 * c, c))

    def backward(tiles):
        return moved(tiles, lambda r, m, c: (r, m - 1 + 2 * c, 1 - c))

    head, tail = forward(head), backward(tail)
    ahead, behind = forward(middle), backward(middle)
    sibling = moved(left, lambda r, m, c: (r, m, 1 - c))
    mirror = gathered(one(received, core), 0, 4)
    own = gathered(received, 4, 2)
    sent = jnp.concatenate([one(own, 2 * (1 - high) + core), one(mirror, 2 - high)], 0)
    across = moved(sent, lambda r, m, c: (r ^ 1, m, c))
    kept_count = out_cols.shape[3]
    partial = products(
        cols,
        kept,
        place,
        centre,
        (own, mirror, left, sibling),
        copy_arrays(centre_copies),
        kept_count,
    )
    head, tail, partial = lax.optimization_barrier((head, tail, partial))
    shared = moved(jnp.concatenate([head, tail], 0), lambda r, m, c: (r, m, 1 - c))
    return products(
        cols,
        kept,
        place,
        outer,
        (own, mirror, across, head, tail, ahead, behind, shared),
        copy_arrays(outer_copies),
        kept_count,
        partial,
    )


def solution(mesh):
    placed = (P("row", "col", None, None, None), P(), P("row", "col", None, None))
    return jax.shard_map(
        on_device,
        mesh=mesh,
        in_specs=placed,
        out_specs=P("row", "col", None, None, None, None),
        check_vma=False,
    )
```
